128 devices in a mesh: heads: 4 (over y_hi, core), ctx: 32 (over z, y_lo, x).
Axes of the slice: x: 4, y: 4 (y_hi: 2, y_lo: 2; y = y_hi * 2 + y_lo), z: 4, core: 2. Of those that a mesh axis runs over, the one named last changes fastest.
Arguments:
- query: bfloat16 [4096, 128, 128], P('ctx', 'heads'), may hold values from -6 to 6
- key: bfloat16 [4096, 8, 128], P('ctx', 'heads'), may hold values from -6 to 6
- value: bfloat16 [4096, 8, 128], P('ctx', 'heads'), may hold values from -6 to 6
- grad_out: bfloat16 [4096, 128, 128], P('ctx', 'heads'), may hold values from -6 to 6
- doc_lengths: int32 [64], replicated, may hold values from 0 to 2304, as said below
- tile_class: int32 [32, 32], replicated, may hold values from 0 to 2, as said below
Outputs:
- attention: bfloat16 [4096, 128, 128], P('ctx', 'heads')
- grad_query: bfloat16 [4096, 128, 128], P('ctx', 'heads')
- grad_key: bfloat16 [4096, 8, 128], P('ctx', 'heads')
- grad_value: bfloat16 [4096, 8, 128], P('ctx', 'heads')
The draws below stay inside these ranges and needn't reach their ends.
Inputs may be any that keep to these rules, and one draw needn't show every extreme that they name: `doc_lengths`: the lengths sum to 4096. One document of exactly 2304 positions starts at a multiple of 256; every other document has at most 256 positions, and every multiple of 256 outside the long document starts a document; empty documents may occur. tile_class[a, b] describes query tile a against key tile b (tiles of 128 positions, documents from doc_lengths): 0 if no query of tile a shares a document with a key of tile b that is not after it (always so where b > a), 2 if b < a and every pair of them does, 1 otherwise.
All inputs are finite; a program needn't handle non-finite values.
Results may differ from the reference program's by a relative error of at most 0.028.
Values may be sent and summed in bfloat16 or wider, within the bound.
No kernel may reach another device: no remote copies, remote signals or barrier semaphores. Data moves between devices by JAX's collectives and lax.ppermute only.
A program may use at most 128 MiB of HBM per device.

```python
import jax
import jax.numpy as jnp
from jax import lax

HQ = 128
KVH = 8
HD = 128
TB = 128
DPG = 4
TOKENS = 4096
SHORT = 256
LONGDOC = 2304
TILES = 32


def doc_layout(base_key):
    slot_count = TOKENS // SHORT
    span = LONGDOC // SHORT
    cut_key, live_key, start_key = jax.random.split(base_key, 3)
    cut_points = jnp.sort(jax.random.randint(cut_key, (slot_count, DPG - 1), 1, SHORT), axis=1)
    live_cuts = jax.random.randint(live_key, (slot_count, 1), 0, DPG)
    cut_points = jnp.where(jnp.arange(DPG - 1)[None, :] < live_cuts, cut_points, SHORT)
    edges = jnp.concatenate([jnp.zeros((slot_count, 1), jnp.int32), cut_points.astype(jnp.int32), jnp.full((slot_count, 1), SHORT, jnp.int32)], axis=1)
    lengths = edges[:, 1:] - edges[:, :-1]
    first = jax.random.randint(start_key, (), 0, slot_count - span + 1)
    slot_ids = jnp.arange(slot_count)[:, None]
    entry_ids = jnp.arange(DPG)[None, :]
    covered = (slot_ids >= first) & (slot_ids < first + span)
    long_entry = jnp.where((slot_ids == first) & (entry_ids == 0), LONGDOC, 0)
    lengths = jnp.where(covered, long_entry, lengths)
    return lengths.reshape(-1).astype(jnp.int32)


def draw_doc_lengths(key, part):
    return doc_layout(key)


def draw_tile_class(key, part):
    lengths = doc_layout(key)
    doc_ends = jnp.cumsum(lengths)
    positions = jnp.arange(TOKENS, dtype=jnp.int32)
    passed = doc_ends[None, :] <= positions[:, None]
    doc_number = jnp.sum(passed.astype(jnp.int32), axis=1)
    doc_start = jnp.max(jnp.where(passed, doc_ends[None, :], 0), axis=1)
    query_tile = jnp.arange(TILES, dtype=jnp.int32)[:, None]
    key_tile = jnp.arange(TILES, dtype=jnp.int32)[None, :]
    query_first = query_tile * TB
    query_last = query_first + TB - 1
    key_first = key_tile * TB
    key_last = key_first + TB - 1
    every_pair = (doc_number[key_first] == doc_number[query_last]) & (key_tile < query_tile)
    any_pair = doc_start[query_first] <= key_last
    classes = jnp.where(every_pair, 2, jnp.where(any_pair, 1, 0))
    classes = jnp.where(key_tile == query_tile, 1, classes)
    return jnp.where(key_tile > query_tile, 0, classes).astype(jnp.int32)


def draw_query(key, part):
    base_key = key
    key = jax.random.fold_in(base_key, 11)
    return jnp.clip(jax.random.normal(key, (TOKENS, HQ, HD), jnp.float32), -6.0, 6.0).astype(jnp.bfloat16)


def draw_key(key, part):
    base_key = key
    key = jax.random.fold_in(base_key, 23)
    return jnp.clip(jax.random.normal(key, (TOKENS, KVH, HD), jnp.float32), -6.0, 6.0).astype(jnp.bfloat16)


def shard_levels(own_key, extent, pieces, least, top_value):
    def one(dim, parts):
        steps = jax.random.uniform(jax.random.fold_in(jax.random.fold_in(own_key, 6), dim), (parts,), jnp.float32, least / len(pieces), top_value / len(pieces))
        return jnp.repeat(jnp.exp(steps), extent[dim] // parts).reshape((-1,) + (1,) * (len(extent) - dim - 1))

    factor_of = one(*pieces[0])
    for cut in pieces[1:]:
        factor_of = factor_of * one(*cut)
    return factor_of


def bell_draw(rng, dims, width, limit, cuts=(), kind=jnp.bfloat16):
    drawn = jax.random.normal(rng, dims, jnp.float32) * width
    if len(cuts) > 0:
        drawn = shard_levels(rng, dims, cuts, -0.22, 0.18) * drawn
    return jnp.clip(drawn, min=-limit, max=limit).astype(kind)


def setup_inputs(seed: int = 0) -> dict:
    splits = jax.random.split(jax.random.key(seed), 7)
    return {
        "query": draw_query(jax.random.fold_in(splits[6], 71), 0),
        "key": draw_key(jax.random.fold_in(splits[6], 71), 0),
        "value": bell_draw(splits[2], (TOKENS, KVH, HD), 1.0, 6.0, ((0, 32), (1, 4))),
        "grad_out": bell_draw(splits[3], (TOKENS, HQ, HD), 1.0, 6.0, ((0, 32), (1, 4))),
        "doc_lengths": draw_doc_lengths(jax.random.fold_in(splits[6], 71), 0),
        "tile_class": draw_tile_class(jax.random.fold_in(splits[6], 71), 0),
    }


MASKED_LOGIT = -1.0e30


def product(form, left, right):
    left, right = lax.optimization_barrier((left, right))
    return jnp.einsum(form, left.astype(jnp.float32), right.astype(jnp.float32))


def keep_state(state):
    return state


def doc_index(doc_ends, positions):
    return jnp.sum((doc_ends[None, :] <= positions[:, None]).astype(jnp.int32), axis=1)


def reference(query, key, value, grad_out, doc_lengths, tile_class):
    ratio = HQ // KVH
    scaling = HD ** -0.5
    doc_ends = jnp.cumsum(doc_lengths).astype(jnp.int32)
    queries = query.reshape(TILES, TB, KVH, ratio, HD)
    cotangents = grad_out.reshape(TILES, TB, KVH, ratio, HD)
    key_tiles = key.reshape(TILES, TB, KVH, HD)
    value_tiles = value.reshape(TILES, TB, KVH, HD)
    tile_rows = jnp.arange(TB, dtype=jnp.int32)

    def tile_step(sums, tile):
        q_tile = queries[tile]
        d_tile = cotangents[tile]
        q_pos = tile * TB + tile_rows
        q_doc = doc_index(doc_ends, q_pos)

        def pair(other):
            k_pos = other * TB + tile_rows
            k_doc = doc_index(doc_ends, k_pos)
            klass = tile_class[tile, other]
            same_doc = (q_doc[:, None] == k_doc[None, :]) & (k_pos[None, :] <= q_pos[:, None])
            allowed = jnp.where(klass == 2, True, jnp.where(klass == 1, same_doc, False))
            logits = product("qgrd,kgd->grqk", q_tile, key_tiles[other]) * scaling
            return jnp.where(allowed[None, None], logits, MASKED_LOGIT), allowed

        def stat_step(other, state):
            def grow(state):
                running, totals = state
                logits = pair(other)[0]
                fresh = jnp.maximum(running, jnp.max(logits, axis=-1))
                totals = totals * jnp.exp(running - fresh) + jnp.sum(jnp.exp(logits - fresh[..., None]), axis=-1)
                return fresh, totals
            return lax.cond(tile_class[tile, other] != 0, grow, keep_state, state)

        start_state = (jnp.full((KVH, ratio, TB), MASKED_LOGIT, jnp.float32), jnp.zeros((KVH, ratio, TB), jnp.float32))
        running, totals = lax.fori_loop(0, tile + 1, stat_step, start_state)
        log_total = running + jnp.log(totals)

        def weights_of(other):
            logits, allowed = pair(other)
            return jnp.where(allowed[None, None], jnp.exp(logits - log_total[..., None]), 0.0)

        def out_step(other, output_sum):
            def add_output(output_sum):
                weights = weights_of(other).astype(jnp.bfloat16)
                return output_sum + product("grqk,kgd->qgrd", weights, value_tiles[other])
            return lax.cond(tile_class[tile, other] != 0, add_output, keep_state, output_sum)

        output_sum = lax.fori_loop(0, tile + 1, out_step, jnp.zeros((TB, KVH, ratio, HD), jnp.float32))
        attention = output_sum.astype(jnp.bfloat16)
        delta = product("qgrd,qgrd->grq", d_tile, attention)

        def back_step(other, state):
            def work(state):
                grad_q, sums = state
                weights = weights_of(other)
                grad_v = product("grqk,qgrd->kgd", weights.astype(jnp.bfloat16), d_tile)
                grad_p = product("qgrd,kgd->grqk", d_tile, value_tiles[other])
                grad_s = (weights * (grad_p - delta[..., None])).astype(jnp.bfloat16)
                grad_q = grad_q + product("grqk,kgd->qgrd", grad_s, key_tiles[other]) * scaling
                grad_k = product("grqk,qgrd->kgd", grad_s, q_tile) * scaling
                current = lax.dynamic_slice_in_dim(sums, other * TB, TB, 1)
                sums = lax.dynamic_update_slice_in_dim(sums, current + jnp.stack((grad_k, grad_v)), other * TB, 1)
                return grad_q, sums
            return lax.cond(tile_class[tile, other] != 0, work, keep_state, state)

        grad_q, sums = lax.fori_loop(0, tile + 1, back_step, (jnp.zeros((TB, KVH, ratio, HD), jnp.float32), sums))
        return sums, (attention, grad_q.astype(jnp.bfloat16))

    sums = jnp.zeros((2, TOKENS, KVH, HD), jnp.float32)
    sums, (attention, grad_q) = lax.scan(tile_step, sums, jnp.arange(TILES, dtype=jnp.int32))
    grads_kv = sums.astype(jnp.bfloat16)
    return (attention.reshape(TOKENS, HQ, HD), grad_q.reshape(TOKENS, HQ, HD), grads_kv[0], grads_kv[1])
```

```python
import functools

import jax
import jax.numpy as jnp
from jax import lax
from jax.experimental import pallas as pl
from jax.experimental.pallas import tpu as pltpu
from jax.sharding import PartitionSpec as P

TB = 128
CHUNK = 2 * TB
NZ, NY, NX = 4, 2, 4
CTX = NZ * NY * NX
HEAVY_CHUNKS = 9
MASKED = -1e30
LOG2E = 1.4426950408889634

F32, BF16 = jnp.float32, jnp.bfloat16


def nt(a, b):
    return lax.dot_general(a, b, (((1,), (1,)), ((), ())), preferred_element_type=F32)


def nn(a, b):
    return lax.dot_general(a, b, (((1,), (0,)), ((), ())), preferred_element_type=F32)


def tn(a, b):
    return lax.dot_general(a, b, (((0,), (0,)), ((), ())), preferred_element_type=F32)


def wide(a):
    return jnp.concatenate([a, a], axis=1)


def attention_kernel(
    meta,
    bias_hbm,
    *refs,
    scaling,
):
    q_in, g_in, k_in, v_in = refs[0:4], refs[4:8], refs[8:12], refs[12:14]
    o_out, dq_out, dk_out, dv_out = refs[14:18], refs[18:22], refs[22:26], refs[26:28]
    (bias, q_s, g_s, k_s, v_s, s_s, mx, stat, delta_s, acc, dq_acc, dk_s, dv_s, o_s, dq_s, dkb, dvb, sems) = refs[28:]
    copies = [(bias_hbm, bias)]
    copies += [(q_in[r], q_s.at[r]) for r in range(NZ)]
    copies += [(k_in[r], k_s.at[pl.ds(8 * r, 8)]) for r in range(NX)]
    copies += [(v_in[r], v_s.at[pl.ds(16 * r, 16)]) for r in range(NY)]
    copies += [(g_in[r], g_s.at[r]) for r in range(NZ)]
    started = []
    for n, (src, dst) in enumerate(copies):
        cp = pltpu.make_async_copy(src, dst, sems.at[n])
        cp.start()
        started.append(cp)
    dk_s[...] = jnp.zeros_like(dk_s)
    dv_s[...] = jnp.zeros_like(dv_s)
    for cp in started:
        cp.wait()
    z, y, x = meta[0], meta[1], meta[2]

    def slots(tile):
        rz = (z - (tile >> 3)) & 3
        ry = y ^ ((tile >> 2) & 1)
        rx = (x - (tile & 3)) & 3
        return rx * 8 + ry * 4 + rz, ry * 16 + rx * 4 + rz

    def chunk_of(ref, pick, chunk):
        return jnp.concatenate(
            [ref[slots(2 * chunk)[pick]], ref[slots(2 * chunk + 1)[pick]]], axis=0
        )

    def add_to(ref, pick, chunk, value):
        first, second = slots(2 * chunk)[pick], slots(2 * chunk + 1)[pick]
        ref[first] += value[:TB]
        ref[second] += value[TB:]

    factor = scaling * LOG2E
    ones = jnp.ones((CHUNK, TB), BF16)

    def task(r, carry):
        first, last = meta[4 + r], meta[8 + r]
        q = q_s[r]
        mx[...] = jnp.full_like(mx, MASKED)

        def logits(chunk):
            return nt(q, chunk_of(k_s, 0, chunk)) * factor

        def keep(chunk, s):
            s_s[chunk - first] = s
            mx[...] = jnp.maximum(mx[...], jnp.maximum(s[:, :TB], s[:, TB:]))

        def visit(chunk, c):
            keep(chunk, logits(chunk))
            return c

        lax.fori_loop(first, last, visit, 0)
        rows = q.shape[0]
        mask = jnp.broadcast_to(bias[r][:, None, :], (TB, rows // TB, CHUNK)).reshape(rows, CHUNK)
        keep(last, logits(last) + mask)
        top = jnp.broadcast_to(jnp.max(mx[...], axis=1, keepdims=True), mx.shape)
        stat[...] = top
        acc[...] = jnp.zeros_like(acc)

        def output(chunk, c):
            p = jnp.exp2(s_s[chunk - first] - wide(stat[...]))
            values = jnp.concatenate([chunk_of(v_s, 1, chunk), ones], axis=1)
            acc[...] += nn(p.astype(BF16), values)
            return c

        lax.fori_loop(first, last + 1, output, 0)
        total = acc[:, TB:]
        out = (acc[:, :TB] / total).astype(BF16)
        o_s[r] = out
        stat[...] = stat[...] + jnp.log2(total)
        g = g_s[r]
        delta = jnp.sum(g.astype(F32) * out.astype(F32), axis=1, keepdims=True)
        delta_s[...] = jnp.broadcast_to(delta, delta_s.shape)
        dq_acc[...] = jnp.zeros_like(dq_acc)

        def back(chunk, c):
            p = jnp.exp2(s_s[chunk - first] - wide(stat[...]))
            add_to(dv_s, 1, chunk, tn(p.astype(BF16), g_s[r]))
            dp = nt(g_s[r], chunk_of(v_s, 1, chunk))
            ds = (p * (dp - wide(delta_s[...]))).astype(BF16)
            dq_acc[...] += nn(ds, chunk_of(k_s, 0, chunk))
            add_to(dk_s, 0, chunk, tn(ds, q_s[r]))
            return c

        lax.fori_loop(first, last + 1, back, 0)
        dq_s[r] = (dq_acc[...] * scaling).astype(BF16)
        return carry

    lax.fori_loop(0, NZ, task, 0)
    dkb[...] = (dk_s[...] * scaling).astype(BF16)
    dvb[...] = dv_s[...].astype(BF16)
    copies = [(dkb.at[pl.ds(8 * r, 8)], dk_out[r]) for r in range(NX)]
    copies += [(dvb.at[pl.ds(16 * r, 16)], dv_out[r]) for r in range(NY)]
    copies += [(o_s.at[r], o_out[r]) for r in range(NZ)]
    copies += [(dq_s.at[r], dq_out[r]) for r in range(NZ)]
    started = []
    for n, (src, dst) in enumerate(copies):
        cp = pltpu.make_async_copy(src, dst, sems.at[n])
        cp.start()
        started.append(cp)
    for cp in started:
        cp.wait()


def attend(meta, bias, qs, gs, ks, vs, scaling):
    rows = qs[0].shape[0]
    width = qs[0].shape[1]
    anywhere = pl.BlockSpec(memory_space=pl.ANY)
    shape = lambda lead: jax.ShapeDtypeStruct((*lead, width), BF16)
    out_shape = [shape((rows,))] * 8 + [shape((8, TB))] * 4 + [shape((16, TB))] * 2
    outs = pl.pallas_call(
        functools.partial(attention_kernel, scaling=scaling),
        out_shape=out_shape,
        in_specs=[pl.BlockSpec(memory_space=pltpu.SMEM)] + [anywhere] * 15,
        out_specs=[anywhere] * 14,
        scratch_shapes=[
            pltpu.VMEM((NZ, TB, CHUNK), F32),
            pltpu.VMEM((NZ, rows, width), BF16),
            pltpu.VMEM((NZ, rows, width), BF16),
            pltpu.VMEM((CTX, TB, width), BF16),
            pltpu.VMEM((CTX, TB, width), BF16),
            pltpu.VMEM((HEAVY_CHUNKS, rows, CHUNK), F32),
            pltpu.VMEM((rows, TB), F32),
            pltpu.VMEM((rows, TB), F32),
            pltpu.VMEM((rows, TB), F32),
            pltpu.VMEM((rows, 2 * width), F32),
            pltpu.VMEM((rows, width), F32),
            pltpu.VMEM((CTX, TB, width), F32),
            pltpu.VMEM((CTX, TB, width), F32),
            pltpu.VMEM((NZ, rows, width), BF16),
            pltpu.VMEM((NZ, rows, width), BF16),
            pltpu.VMEM((CTX, TB, width), BF16),
            pltpu.VMEM((CTX, TB, width), BF16),
            pltpu.SemaphoreType.DMA((16,)),
        ],
        compiler_params=pltpu.CompilerParams(vmem_limit_bytes=60 * 2**20),
        cost_estimate=pl.CostEstimate(
            flops=16 * 12 * rows * CHUNK * width, bytes_accessed=10 * 2**20, transcendentals=0
        ),
        name="attend",
    )(meta, bias, *qs, *gs, *ks, *vs)
    return outs[0:4], outs[4:8], outs[8:12], outs[12:14]


def along_z(a, r):
    return lax.ppermute(a, "ctx", [(i, (i + 8 * r) % CTX) for i in range(CTX)])


def along_x(a, r):
    return lax.ppermute(a, "ctx", [(i, i // NX * NX + (i + r) % NX) for i in range(CTX)])


def along_y(a):
    return lax.ppermute(a, "ctx", [(i, i ^ NX) for i in range(CTX)])


def add_up(*parts):
    total = parts[0].astype(F32)
    for part in parts[1:]:
        total = total + part.astype(F32)
    return total


def on_device(query, key, value, grad_out, doc_lengths, tile_class):
    heads = query.shape[1]
    groups = key.shape[1]
    width = query.shape[2]
    share = heads // NZ
    rows = TB * share
    scaling = width ** (-0.5)
    place = lax.axis_index("ctx")
    z, y, x = place // 8, place // 4 % 2, place % 4

    def group_tile(a, r):
        group = (z + r) % NZ * groups // NZ
        return lax.dynamic_index_in_dim(a, group, 1, keepdims=False)

    def quarter(a, r):
        piece = lax.dynamic_slice_in_dim(a, (z + r) % NZ * share, share, 1)
        return piece.reshape(rows, width)

    kv = [jnp.stack((group_tile(key, r), group_tile(value, r))) for r in range(NZ)]
    kv = [kv[0]] + [along_z(kv[r], r) for r in (1, 2, 3)]
    k_z = jnp.stack([part[0] for part in kv])
    v_z = jnp.stack([part[1] for part in kv])
    qs = [quarter(query, 0)] + [along_z(quarter(query, r), r) for r in (1, 2, 3)]
    gs = [quarter(grad_out, 0)] + [along_z(quarter(grad_out, r), r) for r in (1, 2, 3)]
    k_y = jnp.concatenate((k_z, along_y(k_z)))
    ks = [k_y] + [along_x(k_y, r) for r in (1, 2, 3)]
    v_x = jnp.concatenate([v_z] + [along_x(v_z, r) for r in (1, 2, 3)])
    vs = [v_x, along_y(v_x)]

    doc_ends = jnp.cumsum(doc_lengths)
    tiles = (z - jnp.arange(NZ)) % NZ * 8 + y * 4 + x
    q_pos = tiles[:, None] * TB + jnp.arange(TB)
    k_pos = tiles[:, None] // 2 * CHUNK + jnp.arange(CHUNK)
    q_doc = jnp.sum((doc_ends <= q_pos[..., None]).astype(jnp.int32), axis=-1)
    k_doc = jnp.sum((doc_ends <= k_pos[..., None]).astype(jnp.int32), axis=-1)
    classes = tile_class[tiles]
    last = tiles // 2
    klass = jnp.take_along_axis(classes, k_pos // TB, axis=1)[:, None, :]
    same = (q_doc[:, :, None] == k_doc[:, None, :]) & (k_pos[:, None, :] <= q_pos[:, :, None])
    allowed = (klass == 2) | ((klass == 1) & same)
    bias = jnp.where(allowed, 0.0, MASKED).astype(F32)
    first = (tiles + 1 - jnp.sum((classes != 0).astype(jnp.int32), axis=1)) // 2
    meta = jnp.concatenate([jnp.stack([z, y, x, z]), first, last]).astype(jnp.int32)

    outs, dqs, dks, dvs = attend(meta, bias, qs, gs, ks, vs, scaling)

    def home(parts):
        parts = [parts[0]] + [along_z(parts[r], -r) for r in (1, 2, 3)]
        whole = jnp.stack([part.reshape(TB, share, width) for part in parts], axis=1)
        whole = jnp.roll(whole, z, axis=1)
        return whole.reshape(TB, heads, width)

    attention = home(outs)
    grad_query = home(dqs)

    dk_x = add_up(dks[0], *[along_x(dks[r], -r) for r in (1, 2, 3)])
    dk_y = add_up(dk_x[:NZ], along_y(dk_x[NZ:].astype(BF16)))
    dv_y = add_up(dvs[0], along_y(dvs[1])).reshape(NX, NZ, TB, width)
    dv_x = add_up(dv_y[0], *[along_x(dv_y[r].astype(BF16), -r) for r in (1, 2, 3)])
    dkv = jnp.stack((dk_y, dv_x), axis=1)
    parts = [dkv[0]] + [along_z(dkv[r].astype(BF16), -r) for r in (1, 2, 3)]
    stacked = jnp.stack([part.astype(F32) for part in parts])
    owners = ((z + jnp.arange(NZ)) % NZ * groups) // NZ
    sums = [
        jnp.sum(jnp.where((owners == g)[:, None, None, None], stacked, 0.0), axis=0)
        for g in range(groups)
    ]
    grads = jnp.stack(sums, axis=2).astype(BF16)
    return attention, grad_query, grads[0], grads[1]


def solution(mesh):
    spec = P("ctx", "heads", None)
    return jax.shard_map(
        on_device,
        mesh=mesh,
        in_specs=(spec, spec, spec, spec, P(), P()),
        out_specs=(spec, spec, spec, spec),
        check_vma=False,
    )
```

```python
import functools

import jax
import jax.numpy as jnp
from jax import lax
from jax.experimental import pallas as pl
from jax.experimental.pallas import tpu as pltpu
from jax.sharding import PartitionSpec as P

TB = 128
CHUNK = 2 * TB
NZ, NY, NX = 4, 2, 4
CTX = NZ * NY * NX
MOST_ITEMS = 16
UNROLL = 4
MASKED = -1e30
LOG2E = 1.4426950408889634

F32, BF16 = jnp.float32, jnp.bfloat16


def nt(a, b):
    return lax.dot_general(a, b, (((1,), (1,)), ((), ())), preferred_element_type=F32)


def nn(a, b):
    return lax.dot_general(a, b, (((1,), (0,)), ((), ())), preferred_element_type=F32)


def tn(a, b):
    return lax.dot_general(a, b, (((0,), (0,)), ((), ())), preferred_element_type=F32)


def wide(a):
    return jnp.concatenate([a, a], axis=1)


def attention_kernel(place, classes, lengths, *refs, scaling):
    qg_in, k_in, v_in = refs[0:4], refs[4:9], refs[9:11]
    od_out, dk_out, dv_out = refs[11:15], refs[15:20], refs[20:22]
    (qg_s, k_s, v_s, s_s, top_s, stat, delta_s, acc, dq_acc, dk_s, dv_s, od_s, dkb, dvb, items, sems) = refs[22:]
    rows = qg_s.shape[2]

    low, high = pl.ds(0, NZ), pl.ds(NZ, NZ)

    def column(scratch, r):
        return scratch.at[:, r // 2, r % 2]

    def half(scratch, r, part):
        return scratch.at[part, r // 2, r % 2]

    def v_pieces(outer, scratch):
        return [
            (outer[n].at[pl.ds(NZ * r, NZ)], scratch.at[pl.ds(NZ * n, NZ), r // 2, r % 2])
            for n in range(NY)
            for r in range(NX)
        ]

    def start_all(copies, base):
        started = []
        for n, (src, dst) in enumerate(copies):
            cp = pltpu.make_async_copy(src, dst, sems.at[base + n])
            cp.start()
            started.append(cp)
        return started

    copies = [(k_in[0], column(k_s, 0)), (k_in[1], column(k_s, 1)), (k_in[2], column(k_s, 3))]
    copies += [(k_in[3], half(k_s, 2, low)), (k_in[4], half(k_s, 2, high))]
    copies += [(qg_in[r].at[0], qg_s.at[r, 0]) for r in range(NZ)]
    started_early = start_all(copies, 0)
    copies = v_pieces(v_in, v_s) + [(qg_in[r].at[1], qg_s.at[r, 1]) for r in range(NZ)]
    started_late = start_all(copies, len(started_early))
    me = place[0]
    z, y, x = me >> 3, (me >> 2) & 1, me & 3

    def at(chunk):
        return (y ^ ((chunk >> 1) & 1)) * NZ + (z ^ (chunk >> 2)), (chunk & 1) ^ (x >> 1)

    def chunk_of(ref, chunk):
        return ref[at(chunk)].reshape(CHUNK, ref.shape[-1])

    def add_to(ref, chunk, value):
        ref[at(chunk)] += value.reshape(2, TB, value.shape[-1])

    count = jnp.int32(NZ)
    for r in range(NZ):
        tile = (z ^ r) * 8 + y * 4 + x
        met = sum((classes[tile, b] != 0).astype(jnp.int32) for b in range(classes.shape[1]))
        first, last = (tile + 1 - met) >> 1, tile >> 1
        items[0, r], items[1, r], items[2, r] = jnp.int32(r), last, jnp.int32(0)

        def enlist(n, c, r=r, first=first, count=count):
            items[0, count + n], items[1, count + n], items[2, count + n] = (
                jnp.int32(r),
                first + n,
                jnp.int32(0),
            )
            return c

        lax.fori_loop(0, last - first, enlist, 0)
        count = count + last - first
    for n in range(UNROLL - 1):
        items[0, count + n], items[1, count + n], items[2, count + n] = (
            jnp.int32(0),
            jnp.int32(0),
            jnp.int32(1),
        )

    def steps(body):
        def step(n, c):
            for u in range(UNROLL):
                item = NZ + UNROLL * n + u
                body(item, items[0, item], items[1, item])
            return c

        lax.fori_loop(0, (count - NZ + UNROLL - 1) // UNROLL, step, 0)

    docs = lengths.shape[0]
    spread = jnp.broadcast_to(lengths[...], (docs, docs))
    upto = lax.broadcasted_iota(jnp.int32, (docs, docs), 0) <= lax.broadcasted_iota(
        jnp.int32, (docs, docs), 1
    )
    ends = jnp.sum(jnp.where(upto, spread, 0), axis=0, keepdims=True)
    factor = scaling * LOG2E
    ones = jnp.ones((CHUNK, TB), BF16)

    def mask_of(r):
        tile = (z ^ r) * 8 + y * 4 + x
        last = tile >> 1
        q_pos = tile * TB + lax.broadcasted_iota(jnp.int32, (TB, 1), 0)
        doc_start = jnp.max(jnp.where(ends <= q_pos, ends, 0), axis=1, keepdims=True)
        lane = lax.broadcasted_iota(jnp.int32, (1, CHUNK), 1)
        odd = (lane >> 7) ^ (x & 1)
        k_pos = last * CHUNK + odd * TB + (lane & (TB - 1))
        klass = jnp.where(odd == 0, classes[tile, 2 * last], classes[tile, 2 * last + 1])
        same = (k_pos >= doc_start) & (k_pos <= q_pos)
        allowed = (klass == 2) | ((klass == 1) & same)
        mask = jnp.where(allowed, 0.0, MASKED).astype(F32)
        return jnp.broadcast_to(mask[:, None, :], (TB, rows // TB, CHUNK)).reshape(rows, CHUNK)

    def logits(r, chunk):
        return nt(qg_s[r, 0], chunk_of(k_s, chunk)) * factor

    def tallest(s):
        return jnp.maximum(s[:, :TB], s[:, TB:])

    for cp in started_early:
        cp.wait()

    def own_logits(r):
        s = logits(r, items[1, r]) + mask_of(r)
        s_s[r] = s
        top_s[r] = tallest(s)

    for r in range(NZ):
        own_logits(r)

    def more_logits(item, r, chunk):
        s = logits(r, chunk) + jnp.where(items[2, item] == 1, MASKED, 0.0)
        s_s[item] = s
        top_s[r] = jnp.maximum(top_s[r], tallest(s))

    steps(more_logits)
    dk_s[...] = jnp.zeros_like(dk_s)
    dv_s[...] = jnp.zeros_like(dv_s)
    for cp in started_late:
        cp.wait()

    def weigh(item, r, chunk):
        p = jnp.exp2(s_s[item] - wide(stat[r])).astype(BF16)
        return nn(p, jnp.concatenate([chunk_of(v_s, chunk), ones], axis=1))

    def own_output(r):
        stat[r] = jnp.broadcast_to(jnp.max(top_s[r], axis=1, keepdims=True), stat.shape[1:])
        acc[r] = weigh(r, r, items[1, r])

    for r in range(NZ):
        own_output(r)

    def more_output(item, r, chunk):
        acc[r] += weigh(item, r, chunk)

    steps(more_output)

    def finish(r):
        total = acc[r, :, TB:]
        out = (acc[r, :, :TB] / total).astype(BF16)
        od_s[r, 0] = out
        stat[r] = stat[r] + jnp.log2(total)
        delta = jnp.sum(qg_s[r, 1].astype(F32) * out.astype(F32), axis=1, keepdims=True)
        delta_s[r] = jnp.broadcast_to(delta, delta_s.shape[1:])
        dq_acc[r] = jnp.zeros(dq_acc.shape[1:], F32)

    for r in range(NZ):
        finish(r)
    started = start_all([(od_s.at[r, 0], od_out[r].at[0]) for r in range(NZ)], 0)

    def back(item, r, chunk):
        dp = nt(qg_s[r, 1], chunk_of(v_s, chunk))
        p = jnp.exp2(s_s[item] - wide(stat[r]))
        ds = (p * (dp - wide(delta_s[r]))).astype(BF16)
        add_to(dv_s, chunk, tn(p.astype(BF16), qg_s[r, 1]))
        dq_acc[r] += nn(ds, chunk_of(k_s, chunk))
        add_to(dk_s, chunk, tn(ds, qg_s[r, 0]))

    for r in range(NZ):
        back(r, r, items[1, r])
    steps(back)

    od_s[:, 1] = (dq_acc[...] * scaling).astype(BF16)
    started += start_all([(od_s.at[r, 1], od_out[r].at[1]) for r in range(NZ)], NZ)
    dvb[...] = dv_s[...].astype(BF16)
    started += start_all([(b, a) for a, b in v_pieces(dv_out, dvb)], len(started))
    dkb[...] = (dk_s[...] * scaling).astype(BF16)
    copies = [
        (column(dkb, 0), dk_out[0]),
        (half(dkb, 1, low), dk_out[1].at[low]),
        (half(dkb, 2, low), dk_out[1].at[high]),
        (half(dkb, 3, high), dk_out[2].at[low]),
        (half(dkb, 2, high), dk_out[2].at[high]),
        (half(dkb, 3, low), dk_out[3]),
        (half(dkb, 1, high), dk_out[4]),
    ]
    for cp in started + start_all(copies, len(started)):
        cp.wait()


def attend(place, classes, lengths, qgs, ks, vs, scaling):
    _, rows, width = qgs[0].shape
    anywhere = pl.BlockSpec(memory_space=pl.ANY)
    scalars = pl.BlockSpec(memory_space=pltpu.SMEM)
    shape = lambda *lead: jax.ShapeDtypeStruct((*lead, width), BF16)
    tiles = lambda kind: pltpu.VMEM((NY * NZ, NX // 2, 2, TB, width), kind)
    part = pltpu.VMEM((NZ, 2, rows, width), BF16)
    row = pltpu.VMEM((NZ, rows, TB), F32)
    outs = pl.pallas_call(
        functools.partial(attention_kernel, scaling=scaling),
        out_shape=[shape(2, rows)] * 4 + [shape(8, TB)] * 3 + [shape(4, TB)] * 2 + [shape(16, TB)] * 2,
        in_specs=[scalars, scalars, pl.BlockSpec(memory_space=pltpu.VMEM)] + [anywhere] * 11,
        out_specs=[anywhere] * 11,
        scratch_shapes=[
            part,
            tiles(BF16),
            tiles(BF16),
            pltpu.VMEM((MOST_ITEMS + UNROLL - 1, rows, CHUNK), F32),
            row,
            row,
            row,
            pltpu.VMEM((NZ, rows, 2 * width), F32),
            pltpu.VMEM((NZ, rows, width), F32),
            tiles(F32),
            tiles(F32),
            part,
            tiles(BF16),
            tiles(BF16),
            pltpu.SMEM((3, MOST_ITEMS + UNROLL - 1), jnp.int32),
            pltpu.SemaphoreType.DMA((24,)),
        ],
        compiler_params=pltpu.CompilerParams(vmem_limit_bytes=60 * 2**20),
        cost_estimate=pl.CostEstimate(
            flops=16 * 12 * rows * CHUNK * width, bytes_accessed=10 * 2**20, transcendentals=0
        ),
        name="attend",
    )(place, classes, lengths, *qgs, *ks, *vs)
    return outs[0:4], outs[4:9], outs[9:11]


def split_kernel(place, query, cotangent, *refs):
    outs, (scratch, sems) = refs[:NZ], refs[NZ:]
    z = place[0] >> 3
    share = query.shape[1] // NZ
    for c in range(NZ):
        for n, ref in enumerate((query, cotangent)):
            piece = ref[:, share * c : share * (c + 1), :].astype(F32)
            scratch[z ^ c, n] = piece.reshape(scratch.shape[2:]).astype(BF16)
    copies = [pltpu.make_async_copy(scratch.at[r], outs[r], sems.at[r]) for r in range(NZ)]
    for cp in copies:
        cp.start()
    for cp in copies:
        cp.wait()


def split_heads(place, query, cotangent):
    count, heads, width = query.shape
    lead = (2, count * heads // NZ, width)
    vmem = pl.BlockSpec(memory_space=pltpu.VMEM)
    return pl.pallas_call(
        split_kernel,
        out_shape=[jax.ShapeDtypeStruct(lead, BF16)] * NZ,
        in_specs=[pl.BlockSpec(memory_space=pltpu.SMEM), vmem, vmem],
        out_specs=[pl.BlockSpec(memory_space=pl.ANY)] * NZ,
        scratch_shapes=[pltpu.VMEM((NZ, *lead), BF16), pltpu.SemaphoreType.DMA((NZ,))],
        compiler_params=pltpu.CompilerParams(vmem_limit_bytes=24 * 2**20),
        cost_estimate=pl.CostEstimate(flops=0, bytes_accessed=4 * 2**20, transcendentals=0),
        name="split_heads",
    )(place, query, cotangent)


def join_kernel(place, *refs):
    parts, outs, (scratch, sems) = refs[:NZ], refs[NZ : NZ + 2], refs[NZ + 2 :]
    copies = [pltpu.make_async_copy(parts[r], scratch.at[r], sems.at[r]) for r in range(NZ)]
    for cp in copies:
        cp.start()
    for cp in copies:
        cp.wait()
    z = place[0] >> 3
    count, heads, width = outs[0].shape
    for n, out in enumerate(outs):
        pieces = [
            scratch[z ^ c, n].astype(F32).reshape(count, heads // NZ, width) for c in range(NZ)
        ]
        out[...] = jnp.concatenate(pieces, axis=1).astype(BF16)


def join_heads(place, parts, shape):
    vmem = pl.BlockSpec(memory_space=pltpu.VMEM)
    return pl.pallas_call(
        join_kernel,
        out_shape=[jax.ShapeDtypeStruct(shape, BF16)] * 2,
        in_specs=[pl.BlockSpec(memory_space=pltpu.SMEM)]
        + [pl.BlockSpec(memory_space=pl.ANY)] * NZ,
        out_specs=[vmem, vmem],
        scratch_shapes=[
            pltpu.VMEM((NZ, *parts[0].shape), BF16),
            pltpu.SemaphoreType.DMA((NZ,)),
        ],
        compiler_params=pltpu.CompilerParams(vmem_limit_bytes=24 * 2**20),
        cost_estimate=pl.CostEstimate(flops=0, bytes_accessed=4 * 2**20, transcendentals=0),
        name="join_heads",
    )(place, *parts)


def swap(a, mask):
    return lax.ppermute(a, "ctx", [(i, i ^ mask) for i in range(CTX)])


def along_z(a, r):
    return swap(a, 8 * r)


def along_x(a, r):
    return swap(a, r)


def along_y(a):
    return swap(a, NX)


def add_up(*parts):
    total = parts[0].astype(F32)
    for part in parts[1:]:
        total = total + part.astype(F32)
    return total


def gather_x(a):
    middle = a.shape[0] // 2
    first, third = along_x(a, 1), along_x(a, 3)
    return a, first, third, along_x(third[:middle], 1), along_x(first[middle:], 3)


def reduce_x(own, to_first, to_third, later_third, later_first):
    middle = own.shape[0] // 2
    from_first, from_third = along_x(to_first, 1), along_x(to_third, 3)
    low = along_x(add_up(later_third, from_first[middle:]).astype(BF16), 3)
    high = along_x(add_up(later_first, from_third[middle:]).astype(BF16), 1)
    return (
        add_up(own[:middle], from_first[:middle], low),
        add_up(own[middle:], from_third[:middle], high),
    )


def on_device(query, key, value, grad_out, doc_lengths, tile_class):
    groups = key.shape[1]
    width = query.shape[2]
    scaling = width ** (-0.5)
    place = lax.axis_index("ctx")
    z = place // 8

    here = place.reshape(1).astype(jnp.int32)

    def group_tile(a, r):
        return lax.dynamic_index_in_dim(a, (z ^ r) * groups // NZ, 1, keepdims=False)

    others = (1, 2, 3)
    kv = [jnp.stack((group_tile(key, r), group_tile(value, r))) for r in range(NZ)]
    qgs = split_heads(here, query, grad_out)
    kv, qgs = lax.optimization_barrier((kv, qgs))
    kv = [kv[0]] + [along_z(kv[r], r) for r in others]
    qg_near = {r: along_z(qgs[r], r) for r in (1, 3)}
    k_z = jnp.stack([part[0] for part in kv])
    v_z = jnp.stack([part[1] for part in kv])
    k_y = jnp.concatenate((k_z, along_y(k_z)))
    v_own, v_1, v_3, v_2a, v_2b = gather_x(v_z)
    v_x = jnp.concatenate((v_own, v_1, v_2a, v_2b, v_3))
    k_y, v_x, qg_near, qg_far = lax.optimization_barrier((k_y, v_x, qg_near, qgs[2]))
    ks = gather_x(k_y)
    vs = [v_x, along_y(v_x)]
    qgs = [qgs[0], qg_near[1], along_z(qg_far, 2), qg_near[3]]

    ods, dks, dvs = attend(here, tile_class, doc_lengths.reshape(-1, 1), qgs, ks, vs, scaling)

    dk_low, dk_high = reduce_x(*dks)
    dv_y = add_up(dvs[0], along_y(dvs[1])).reshape(NX, NZ, TB, width)
    od_near = {r: along_z(ods[r], r) for r in (1, 3)}
    dk_y = add_up(dk_low, along_y(dk_high.astype(BF16)))
    dv_b = dv_y.astype(BF16)
    dv_y, dv_b, od_near, od_far = lax.optimization_barrier((dv_y, dv_b, od_near, ods[2]))
    od_far = along_z(od_far, 2)
    dv_x = reduce_x(
        dv_y[0],
        jnp.concatenate((dv_b[1, :2], dv_b[2, :2])),
        jnp.concatenate((dv_b[3, 2:], dv_b[2, 2:])),
        dv_y[3, :2],
        dv_y[1, 2:],
    )
    dkv = jnp.stack((dk_y, jnp.concatenate(dv_x)), axis=1)
    dkv, od_far = lax.optimization_barrier((dkv, od_far))
    parts = [dkv[0]] + [along_z(dkv[r].astype(BF16), r).astype(F32) for r in others]
    attention, grad_query = join_heads(here, [ods[0], od_near[1], od_far, od_near[3]], query.shape)
    mine = (parts[0] + parts[1]).astype(BF16)[:, :, None, :]
    other = (parts[2] + parts[3]).astype(BF16)[:, :, None, :]
    group = lax.broadcasted_iota(jnp.int32, (1, 1, groups, 1), 2)
    grads = jnp.where(group == z * groups // NZ, mine, other)
    return attention, grad_query, grads[0], grads[1]


def solution(mesh):
    spec = P("ctx", "heads", None)
    return jax.shard_map(
        on_device,
        mesh=mesh,
        in_specs=(spec, spec, spec, spec, P(), P()),
        out_specs=(spec, spec, spec, spec),
        check_vma=False,
    )
```

```python
import functools

import jax
import jax.numpy as jnp
from jax import lax
from jax.experimental import pallas as pl
from jax.experimental.pallas import tpu as pltpu
from jax.sharding import PartitionSpec as P

TB = 128
CHUNK = 2 * TB
NZ, NY, NX = 4, 2, 4
CTX = NZ * NY * NX
MOST_ITEMS = 16
SLOTS = 10
UNROLL = 4
MASKED = -1e30
LOG2E = 1.4426950408889634

F32, BF16 = jnp.float32, jnp.bfloat16


def nt(a, b):
    return lax.dot_general(a, b, (((1,), (1,)), ((), ())), preferred_element_type=F32)


def nn(a, b):
    return lax.dot_general(a, b, (((1,), (0,)), ((), ())), preferred_element_type=F32)


def tn(a, b):
    return lax.dot_general(a, b, (((0,), (0,)), ((), ())), preferred_element_type=F32)


def wide(a):
    return jnp.concatenate([a, a], axis=1)


def first_layer(start, y, x):
    return (start - (y * NX + x) + 7) >> 3


def long_start(sizes):
    def step(n, c):
        seen, start = c
        return seen + sizes[n], jnp.where(sizes[n] > CHUNK, seen, start)

    zero = jnp.int32(0)
    return lax.fori_loop(0, sizes.shape[0], step, (zero, zero), unroll=8)[1] // TB


def layers(start, y, x):
    z0 = first_layer(start, y, x)
    return jnp.where(z0 == 0, 2, 0), jnp.where(z0 == 2, 1, 3), z0, z0 + 1


def attention_kernel(place, first_tile, classes, lengths, *refs, scaling):
    qg_in, own_in, (first_in, third_in, far_in, further_in, across_in) = (
        refs[0],
        refs[1:5],
        refs[5:10],
    )
    od_out, (own_out, first_out, third_out, later_third, later_first, across_out), layers_out = (
        refs[10],
        refs[11:17],
        refs[17],
    )
    (qg_s, kv_s, s_s, top_s, stat, delta_s, acc, dq_acc, dkv_s, od_s, dkvb, items, sems) = refs[18:]
    rows = qg_s.shape[2]
    me, start = place[0], first_tile[0]
    z, y, x = me >> 3, (me >> 2) & 1, me & 3

    def start_all(copies, base):
        started = []
        for n, (src, dst) in enumerate(copies):
            cp = pltpu.make_async_copy(src, dst, sems.at[base + n])
            cp.start()
            started.append(cp)
        return started

    order = layers(start, y, x)
    copies = [(own_in[r], kv_s.at[r, 0]) for r in range(NZ)]
    copies += [(first_in.at[n], kv_s.at[z ^ order[n], 1]) for n in range(NZ)]
    copies += [
        (first_in.at[pl.ds(4, 2)], kv_s.at[pl.ds(6, 2), 1]),
        (third_in.at[pl.ds(0, 2)], kv_s.at[pl.ds(4, 2), 1]),
        (third_in.at[pl.ds(2, 2)], kv_s.at[pl.ds(8, 2), 1]),
        (far_in, kv_s.at[pl.ds(4, 2), 0]),
        (further_in, kv_s.at[pl.ds(8, 2), 0]),
        (across_in, kv_s.at[pl.ds(6, 2), 0]),
    ]
    copies += [(qg_in.at[:, 0], qg_s.at[:, 0])]
    started_early = start_all(copies, 0)
    copies = [(qg_in.at[:, 1], qg_s.at[:, 1])]
    started_late = start_all(copies, len(started_early))
    def slot_of(chunk):
        there_y, there_x = (chunk >> 1) & 1, chunk & 1
        pair = (y ^ there_y) * 2 + (there_x ^ (x >> 1))
        layer = (chunk >> 2) - first_layer(start, there_y, 2 * there_x)
        return jnp.where(pair == 0, z ^ (chunk >> 2), 2 + 2 * pair + layer)

    def chunk_of(kind, chunk):
        return kv_s[slot_of(chunk), :, kind].reshape(CHUNK, kv_s.shape[-1])

    def add_to(kind, chunk, value):
        dkv_s[slot_of(chunk), :, kind] += value.reshape(2, TB, value.shape[-1])

    count = jnp.int32(NZ)
    for r in range(NZ):
        tile = r * 8 + y * 4 + x
        met = sum((classes[tile, b] != 0).astype(jnp.int32) for b in range(classes.shape[1]))
        first, last = (tile + 1 - met) >> 1, tile >> 1
        items[0, r], items[1, r], items[2, r] = jnp.int32(r), last, jnp.int32(0)

        def enlist(n, c, r=r, first=first, count=count):
            items[0, count + n], items[1, count + n], items[2, count + n] = (
                jnp.int32(r),
                first + n,
                jnp.int32(0),
            )
            return c

        lax.fori_loop(0, last - first, enlist, 0)
        count = count + last - first
    for n in range(UNROLL - 1):
        items[0, count + n], items[1, count + n], items[2, count + n] = (
            jnp.int32(0),
            items[1, 0],
            jnp.int32(1),
        )

    def steps(body):
        def step(n, c):
            for u in range(UNROLL):
                item = NZ + UNROLL * n + u
                body(item, items[0, item], items[1, item])
            return c

        lax.fori_loop(0, (count - NZ + UNROLL - 1) // UNROLL, step, 0)

    docs = lengths.shape[0]
    spread = jnp.broadcast_to(lengths[...], (docs, docs))
    upto = lax.broadcasted_iota(jnp.int32, (docs, docs), 0) <= lax.broadcasted_iota(
        jnp.int32, (docs, docs), 1
    )
    ends = jnp.sum(jnp.where(upto, spread, 0), axis=0, keepdims=True)
    factor = scaling * LOG2E
    ones = jnp.ones((CHUNK, TB), BF16)

    def mask_of(r):
        tile = r * 8 + y * 4 + x
        last = tile >> 1
        q_pos = tile * TB + lax.broadcasted_iota(jnp.int32, (TB, 1), 0)
        doc_start = jnp.max(jnp.where(ends <= q_pos, ends, 0), axis=1, keepdims=True)
        lane = lax.broadcasted_iota(jnp.int32, (1, CHUNK), 1)
        odd = (lane >> 7) ^ (x & 1)
        k_pos = last * CHUNK + odd * TB + (lane & (TB - 1))
        klass = jnp.where(odd == 0, classes[tile, 2 * last], classes[tile, 2 * last + 1])
        same = (k_pos >= doc_start) & (k_pos <= q_pos)
        allowed = (klass == 2) | ((klass == 1) & same)
        mask = jnp.where(allowed, 0.0, MASKED).astype(F32)
        return jnp.broadcast_to(mask[:, None, :], (TB, rows // TB, CHUNK)).reshape(rows, CHUNK)

    def logits(r, chunk):
        return nt(qg_s[r, 0], chunk_of(0, chunk)) * factor

    def tallest(s):
        return jnp.maximum(s[:, :TB], s[:, TB:])

    for r in range(NZ):
        layers_out[r] = (z ^ r) - first_layer(start, y, x)
    for cp in started_early:
        cp.wait()

    def own_logits(r):
        s = logits(r, items[1, r]) + mask_of(r)
        s_s[r] = s
        top_s[r] = tallest(s)

    for r in range(NZ):
        own_logits(r)

    def more_logits(item, r, chunk):
        s = logits(r, chunk) + jnp.where(items[2, item] == 1, MASKED, 0.0)
        s_s[item] = s
        top_s[r] = jnp.maximum(top_s[r], tallest(s))

    steps(more_logits)
    dkv_s[...] = jnp.zeros_like(dkv_s)
    for cp in started_late:
        cp.wait()

    def weigh(item, r, chunk):
        p = jnp.exp2(s_s[item] - wide(stat[r])).astype(BF16)
        return nn(p, jnp.concatenate([chunk_of(1, chunk), ones], axis=1))

    def own_output(r):
        stat[r] = jnp.broadcast_to(jnp.max(top_s[r], axis=1, keepdims=True), stat.shape[1:])
        acc[r] = weigh(r, r, items[1, r])

    for r in range(NZ):
        own_output(r)

    def more_output(item, r, chunk):
        acc[r] += weigh(item, r, chunk)

    steps(more_output)

    def finish(r):
        total = acc[r, :, TB:]
        out = (acc[r, :, :TB] / total).astype(BF16)
        od_s[r, 0] = out
        stat[r] = stat[r] + jnp.log2(total)
        delta = jnp.sum(qg_s[r, 1].astype(F32) * out.astype(F32), axis=1, keepdims=True)
        delta_s[r] = jnp.broadcast_to(delta, delta_s.shape[1:])
        dq_acc[r] = jnp.zeros(dq_acc.shape[1:], F32)

    for r in range(NZ):
        finish(r)
    started = start_all([(od_s.at[:, 0], od_out.at[:, 0])], 0)

    def back(item, r, chunk):
        dp = nt(qg_s[r, 1], chunk_of(1, chunk))
        p = jnp.exp2(s_s[item] - wide(stat[r]))
        ds = (p * (dp - wide(delta_s[r]))).astype(BF16)
        add_to(1, chunk, tn(p.astype(BF16), qg_s[r, 1]))
        dq_acc[r] += nn(ds, chunk_of(0, chunk))
        add_to(0, chunk, tn(ds, qg_s[r, 0]))

    for r in range(NZ):
        back(r, r, items[1, r])
    steps(back)

    od_s[:, 1] = (dq_acc[...] * scaling).astype(BF16)
    started += start_all([(od_s.at[:, 1], od_out.at[:, 1])], 1)
    dkvb[:, :, 0] = (dkv_s[:, :, 0] * scaling).astype(BF16)
    dkvb[:, :, 1] = dkv_s[:, :, 1].astype(BF16)
    copies = [
        (dkvb.at[pl.ds(0, 4), 1], first_out.at[pl.ds(0, 4)]),
        (dkvb.at[pl.ds(4, 2), 0], first_out.at[pl.ds(4, 2)]),
        (dkvb.at[pl.ds(8, 2), 1], third_out.at[pl.ds(0, 2)]),
        (dkvb.at[pl.ds(8, 2), 0], third_out.at[pl.ds(2, 2)]),
        (dkvb.at[pl.ds(4, 2), 1], later_third),
        (dkvb.at[pl.ds(6, 2), 1], later_first),
        (dkvb.at[pl.ds(6, 2), 0], across_out),
        (dkvb.at[pl.ds(0, 4), 0], own_out),
    ]
    for cp in started + start_all(copies, len(started)):
        cp.wait()


def attend(place, start, classes, lengths, qg, kvs, scaling):
    _, _, rows, width = qg.shape
    anywhere = pl.BlockSpec(memory_space=pl.ANY)
    scalars = pl.BlockSpec(memory_space=pltpu.SMEM)
    shape = lambda *lead: jax.ShapeDtypeStruct((*lead, width), BF16)
    slots = lambda kind: pltpu.VMEM((SLOTS, 2, 2, TB, width), kind)
    part = pltpu.VMEM((NZ, 2, rows, width), BF16)
    row = pltpu.VMEM((NZ, rows, TB), F32)
    outs = pl.pallas_call(
        functools.partial(attention_kernel, scaling=scaling),
        out_shape=[shape(NZ, 2, rows)]
        + [shape(n, 2, TB) for n in (4, 6, 4, 2, 2, 2)]
        + [jax.ShapeDtypeStruct((NZ,), jnp.int32)],
        in_specs=[scalars] * 3 + [pl.BlockSpec(memory_space=pltpu.VMEM)] + [anywhere] * 10,
        out_specs=[anywhere] * 7 + [scalars],
        scratch_shapes=[
            part,
            slots(BF16),
            pltpu.VMEM((MOST_ITEMS + UNROLL - 1, rows, CHUNK), F32),
            row,
            row,
            row,
            pltpu.VMEM((NZ, rows, 2 * width), F32),
            pltpu.VMEM((NZ, rows, width), F32),
            slots(F32),
            part,
            slots(BF16),
            pltpu.SMEM((3, MOST_ITEMS + UNROLL - 1), jnp.int32),
            pltpu.SemaphoreType.DMA((24,)),
        ],
        compiler_params=pltpu.CompilerParams(vmem_limit_bytes=60 * 2**20),
        cost_estimate=pl.CostEstimate(
            flops=16 * 12 * rows * CHUNK * width, bytes_accessed=10 * 2**20, transcendentals=0
        ),
        name="attend",
    )(place, start, classes, lengths.reshape(-1, 1), qg, *kvs)
    return outs[0], outs[1:7], outs[7]


def pick_kernel(place, key, value, *outs):
    z = place[0] >> 3
    groups = key.shape[1]
    for n, ref in enumerate((key, value)):
        whole = ref[...].astype(F32)
        kinds = [whole[:, g, :] for g in range(groups)]
        for r in range(NZ):
            piece = kinds[0]
            for g in range(1, groups):
                piece = jnp.where((z ^ r) * groups // NZ == g, kinds[g], piece)
            outs[r][n] = piece.astype(BF16)


def pick_groups(place, key, value):
    vmem = pl.BlockSpec(memory_space=pltpu.VMEM)
    return pl.pallas_call(
        pick_kernel,
        out_shape=[jax.ShapeDtypeStruct((2, key.shape[0], key.shape[2]), BF16)] * NZ,
        in_specs=[pl.BlockSpec(memory_space=pltpu.SMEM), vmem, vmem],
        out_specs=[vmem] * NZ,
        compiler_params=pltpu.CompilerParams(vmem_limit_bytes=4 * 2**20),
        cost_estimate=pl.CostEstimate(flops=0, bytes_accessed=2**19, transcendentals=0),
        name="pick_groups",
    )(place, key, value)


def arrange_kernel(place, sizes, *refs):
    parts, (whole, chosen, first_tile), sems = refs[:NZ], refs[NZ : NZ + 3], refs[NZ + 3]
    me, start = place[0], long_start(sizes)
    first_tile[0] = start
    z, y, x = me >> 3, (me >> 2) & 1, me & 3
    order = layers(start, y, x)
    copies = []
    for r in range(NZ):
        there = z ^ r
        spot = sum(jnp.where(there == order[n], n, 0) for n in range(1, NZ))
        copies.append(pltpu.make_async_copy(parts[r], whole.at[spot], sems.at[r]))
        copies[-1].start()
        picked = (there == order[2]) | (there == order[3])

        @pl.when(picked)
        def _(r=r, spot=spot):
            cp = pltpu.make_async_copy(parts[r], chosen.at[jnp.maximum(spot - 2, 0)], sems.at[NZ])
            cp.start()
            cp.wait()

    for cp in copies:
        cp.wait()


def arrange(place, lengths, parts):
    shape = lambda n: jax.ShapeDtypeStruct((n, *parts[0].shape), BF16)
    return pl.pallas_call(
        arrange_kernel,
        out_shape=[shape(4), shape(2), jax.ShapeDtypeStruct((1,), jnp.int32)],
        in_specs=[pl.BlockSpec(memory_space=pltpu.SMEM)] * 2
        + [pl.BlockSpec(memory_space=pltpu.VMEM)] * NZ,
        out_specs=[pl.BlockSpec(memory_space=pl.ANY)] * 2
        + [pl.BlockSpec(memory_space=pltpu.SMEM)],
        scratch_shapes=[pltpu.SemaphoreType.DMA((NZ + 1,))],
        compiler_params=pltpu.CompilerParams(vmem_limit_bytes=4 * 2**20),
        cost_estimate=pl.CostEstimate(flops=0, bytes_accessed=2**19, transcendentals=0),
        name="arrange",
    )(place, lengths, *parts)


def split_kernel(query, cotangent, out):
    share = query.shape[1] // NZ
    for c in range(NZ):
        for n, ref in enumerate((query, cotangent)):
            piece = ref[:, share * c : share * (c + 1), :].astype(F32)
            out[c, n] = piece.reshape(out.shape[2:]).astype(BF16)


def split_heads(query, cotangent):
    count, heads, width = query.shape
    return pl.pallas_call(
        split_kernel,
        out_shape=jax.ShapeDtypeStruct((NZ, 2, count * heads // NZ, width), BF16),
        compiler_params=pltpu.CompilerParams(vmem_limit_bytes=24 * 2**20),
        cost_estimate=pl.CostEstimate(flops=0, bytes_accessed=4 * 2**20, transcendentals=0),
        name="split_heads",
    )(query, cotangent)


def join_kernel(parts, *outs):
    count, heads, width = outs[0].shape
    for n, out in enumerate(outs):
        pieces = [parts[c, n].astype(F32).reshape(count, heads // NZ, width) for c in range(NZ)]
        out[...] = jnp.concatenate(pieces, axis=1).astype(BF16)


def join_heads(parts, shape):
    return pl.pallas_call(
        join_kernel,
        out_shape=[jax.ShapeDtypeStruct(shape, BF16)] * 2,
        compiler_params=pltpu.CompilerParams(vmem_limit_bytes=24 * 2**20),
        cost_estimate=pl.CostEstimate(flops=0, bytes_accessed=4 * 2**20, transcendentals=0),
        name="join_heads",
    )(parts)


def swap(a, mask):
    return lax.ppermute(a, "ctx", [(i, i ^ mask) for i in range(CTX)])


def along_z(a, r):
    return swap(a, 8 * r)


def exchange_z(a):
    groups = [list(range(first, CTX, NY * NX)) for first in range(NY * NX)]
    return lax.all_to_all(a, "ctx", 0, 0, axis_index_groups=groups, tiled=True)


def along_x(a, r):
    return swap(a, r)


def along_y(a):
    return swap(a, NX)


def add_up(*parts):
    total = parts[0].astype(F32)
    for part in parts[1:]:
        total = total + part.astype(F32)
    return total


def on_device(query, key, value, grad_out, doc_lengths, tile_class):
    groups = key.shape[1]
    width = query.shape[2]
    scaling = width ** (-0.5)
    place = lax.axis_index("ctx")
    z = place // 8

    here = place.reshape(1).astype(jnp.int32)

    others = (1, 2, 3)
    kv = pick_groups(here, key, value)
    qg = split_heads(query, grad_out)
    kv = [kv[0]] + [along_z(kv[r], r) for r in others]
    whole, chosen, start = arrange(here, doc_lengths, kv)
    chosen, qg = lax.optimization_barrier((chosen, qg))
    qg = exchange_z(qg)
    across = along_y(chosen)
    first = along_x(jnp.concatenate((whole, across)), 1)
    third = along_x(jnp.concatenate((chosen, across)), 3)
    far, further = along_x(third[:2], 1), along_x(first[4:], 3)

    od, dkvs, layer = attend(
        here, start, tile_class, doc_lengths, qg, [*kv, first, third, far, further, across], scaling
    )

    own, to_first, to_third, later_third, later_first, own_across = dkvs
    from_first, from_third = along_x(to_first, 1), along_x(to_third, 3)
    od = exchange_z(od)
    to_third = add_up(later_third, from_first[4:]).astype(BF16)
    to_first = add_up(later_first, from_third[2:]).astype(BF16)
    more, more_across = along_x(to_third, 3), along_x(to_first, 1)
    across = along_y(add_up(own_across, from_third[:2], more_across).astype(BF16))
    chosen = add_up(more, across)
    layer = layer[:, None, None, None]
    dkv = add_up(own, from_first[:4]) + jnp.where(
        layer == 0, chosen[0], jnp.where(layer == 1, chosen[1], 0.0)
    )
    parts = [dkv[0]] + [along_z(dkv[r].astype(BF16), r).astype(F32) for r in others]
    attention, grad_query = join_heads(od, query.shape)
    mine = (parts[0] + parts[1]).astype(BF16)[:, :, None, :]
    other = (parts[2] + parts[3]).astype(BF16)[:, :, None, :]
    group = lax.broadcasted_iota(jnp.int32, (1, 1, groups, 1), 2)
    grads = jnp.where(group == z * groups // NZ, mine, other)
    return attention, grad_query, grads[0], grads[1]


def solution(mesh):
    spec = P("ctx", "heads", None)
    return jax.shard_map(
        on_device,
        mesh=mesh,
        in_specs=(spec, spec, spec, spec, P(), P()),
        out_specs=(spec, spec, spec, spec),
        check_vma=False,
    )
```

```python
import functools

import jax
import jax.numpy as jnp
from jax import lax
from jax.experimental import pallas as pl
from jax.experimental.pallas import tpu as pltpu
from jax.sharding import PartitionSpec as P

TB = 128
CHUNK = 2 * TB
NZ, NY, NX = 4, 2, 4
CTX = NZ * NY * NX
MOST_ITEMS = 16
SLOTS = 10
UNROLL = 4
MASKED = -1e30
LOG2E = 1.4426950408889634

F32, BF16 = jnp.float32, jnp.bfloat16


def nt(a, b):
    return lax.dot_general(a, b, (((1,), (1,)), ((), ())), preferred_element_type=F32)


def nn(a, b):
    return lax.dot_general(a, b, (((1,), (0,)), ((), ())), preferred_element_type=F32)


def tn(a, b):
    return lax.dot_general(a, b, (((0,), (0,)), ((), ())), preferred_element_type=F32)


def wide(a):
    return jnp.concatenate([a, a], axis=1)


def first_layer(start, y, x):
    return (start - (y * NX + x) + 7) >> 3


def long_start(sizes):
    def step(n, c):
        seen, start = c
        return seen + sizes[n], jnp.where(sizes[n] > CHUNK, seen, start)

    zero = jnp.int32(0)
    return lax.fori_loop(0, sizes.shape[0], step, (zero, zero), unroll=8)[1] // TB


def layers(start, y, x):
    z0 = first_layer(start, y, x)
    return jnp.where(z0 == 0, 2, 0), jnp.where(z0 == 2, 1, 3), z0, z0 + 1


def attention_kernel(place, first_tile, classes, lengths, *refs, scaling):
    qg_in, own_in, (first_in, third_in, far_in, further_in, across_in) = (
        refs[0],
        refs[1:5],
        refs[5:10],
    )
    od_out, (own_out, first_out, third_out, later_third, later_first, across_out), layers_out = (
        refs[10],
        refs[11:17],
        refs[17],
    )
    (qg_s, kv_s, s_s, top_s, stat, delta_s, acc, dq_acc, dkv_s, od_s, dkvb, items, sems) = refs[18:]
    rows = qg_s.shape[2]
    me, start = place[0], first_tile[0]
    z, y, x = me >> 3, (me >> 2) & 1, me & 3

    def start_all(copies, base):
        started = []
        for n, (src, dst) in enumerate(copies):
            cp = pltpu.make_async_copy(src, dst, sems.at[base + n])
            cp.start()
            started.append(cp)
        return started

    order = layers(start, y, x)
    copies = [(own_in[r], kv_s.at[r, 0]) for r in range(NZ)]
    copies += [(first_in.at[n], kv_s.at[z ^ order[n], 1]) for n in range(NZ)]
    copies += [
        (first_in.at[pl.ds(4, 2)], kv_s.at[pl.ds(6, 2), 1]),
        (third_in.at[pl.ds(0, 2)], kv_s.at[pl.ds(4, 2), 1]),
        (third_in.at[pl.ds(2, 2)], kv_s.at[pl.ds(8, 2), 1]),
        (far_in, kv_s.at[pl.ds(4, 2), 0]),
        (further_in, kv_s.at[pl.ds(8, 2), 0]),
        (across_in, kv_s.at[pl.ds(6, 2), 0]),
    ]
    copies += [(qg_in.at[:, 0], qg_s.at[:, 0])]
    started_early = start_all(copies, 0)
    copies = [(qg_in.at[:, 1], qg_s.at[:, 1])]
    started_late = start_all(copies, len(started_early))
    def slot_of(chunk):
        there_y, there_x = (chunk >> 1) & 1, chunk & 1
        pair = (y ^ there_y) * 2 + (there_x ^ (x >> 1))
        layer = (chunk >> 2) - first_layer(start, there_y, 2 * there_x)
        return jnp.where(pair == 0, z ^ (chunk >> 2), 2 + 2 * pair + layer)

    def chunk_of(kind, chunk):
        return kv_s[slot_of(chunk), :, kind].reshape(CHUNK, kv_s.shape[-1])

    def add_to(kind, chunk, value):
        dkv_s[slot_of(chunk), :, kind] += value.reshape(2, TB, value.shape[-1])

    count = jnp.int32(NZ)
    for r in range(NZ):
        tile = r * 8 + y * 4 + x
        met = sum((classes[tile, b] != 0).astype(jnp.int32) for b in range(classes.shape[1]))
        first, last = (tile + 1 - met) >> 1, tile >> 1
        items[0, r], items[1, r], items[2, r] = jnp.int32(r), last, jnp.int32(0)

        def enlist(n, c, r=r, first=first, count=count):
            items[0, count + n], items[1, count + n], items[2, count + n] = (
                jnp.int32(r),
                first + n,
                jnp.int32(0),
            )
            return c

        lax.fori_loop(0, last - first, enlist, 0)
        count = count + last - first
    for n in range(UNROLL - 1):
        items[0, count + n], items[1, count + n], items[2, count + n] = (
            jnp.int32(0),
            items[1, 0],
            jnp.int32(1),
        )

    def steps(body):
        def step(n, c):
            for u in range(UNROLL):
                item = NZ + UNROLL * n + u
                body(item, items[0, item], items[1, item])
            return c

        lax.fori_loop(0, (count - NZ + UNROLL - 1) // UNROLL, step, 0)

    docs = lengths.shape[0]
    spread = jnp.broadcast_to(lengths[...], (docs, docs))
    upto = lax.broadcasted_iota(jnp.int32, (docs, docs), 0) <= lax.broadcasted_iota(
        jnp.int32, (docs, docs), 1
    )
    ends = jnp.sum(jnp.where(upto, spread, 0), axis=0, keepdims=True)
    factor = scaling * LOG2E
    ones = jnp.ones((CHUNK, TB), BF16)

    def mask_of(r):
        tile = r * 8 + y * 4 + x
        last = tile >> 1
        q_pos = tile * TB + lax.broadcasted_iota(jnp.int32, (TB, 1), 0)
        doc_start = jnp.max(jnp.where(ends <= q_pos, ends, 0), axis=1, keepdims=True)
        lane = lax.broadcasted_iota(jnp.int32, (1, CHUNK), 1)
        odd = (lane >> 7) ^ (x & 1)
        k_pos = last * CHUNK + odd * TB + (lane & (TB - 1))
        klass = jnp.where(odd == 0, classes[tile, 2 * last], classes[tile, 2 * last + 1])
        same = (k_pos >= doc_start) & (k_pos <= q_pos)
        allowed = (klass == 2) | ((klass == 1) & same)
        mask = jnp.where(allowed, 0.0, MASKED).astype(F32)
        return jnp.broadcast_to(mask[:, None, :], (TB, rows // TB, CHUNK)).reshape(rows, CHUNK)

    def logits(r, chunk):
        return nt(qg_s[r, 0], chunk_of(0, chunk)) * factor

    def tallest(s):
        return jnp.maximum(s[:, :TB], s[:, TB:])

    for r in range(NZ):
        layers_out[r] = (z ^ r) - first_layer(start, y, x)
    for cp in started_early:
        cp.wait()

    def own_logits(r):
        s = logits(r, items[1, r]) + mask_of(r)
        s_s[r] = s
        top_s[r] = tallest(s)

    for r in range(NZ):
        own_logits(r)

    def more_logits(item, r, chunk):
        s = logits(r, chunk) + jnp.where(items[2, item] == 1, MASKED, 0.0)
        s_s[item] = s
        top_s[r] = jnp.maximum(top_s[r], tallest(s))

    steps(more_logits)
    dkv_s[...] = jnp.zeros_like(dkv_s)
    for cp in started_late:
        cp.wait()

    def weigh(item, r, chunk):
        p = jnp.exp2(s_s[item] - wide(stat[r])).astype(BF16)
        return nn(p, jnp.concatenate([chunk_of(1, chunk), ones], axis=1))

    def own_output(r):
        stat[r] = jnp.broadcast_to(jnp.max(top_s[r], axis=1, keepdims=True), stat.shape[1:])
        acc[r] = weigh(r, r, items[1, r])

    for r in range(NZ):
        own_output(r)

    def more_output(item, r, chunk):
        acc[r] += weigh(item, r, chunk)

    steps(more_output)

    def finish(r):
        total = acc[r, :, TB:]
        out = (acc[r, :, :TB] / total).astype(BF16)
        od_s[r, 0] = out
        stat[r] = stat[r] + jnp.log2(total)
        delta = jnp.sum(qg_s[r, 1].astype(F32) * out.astype(F32), axis=1, keepdims=True)
        delta_s[r] = jnp.broadcast_to(delta, delta_s.shape[1:])
        dq_acc[r] = jnp.zeros(dq_acc.shape[1:], F32)

    for r in range(NZ):
        finish(r)
    started = start_all([(od_s.at[:, 0], od_out.at[:, 0])], 0)

    def back(item, r, chunk):
        dp = nt(qg_s[r, 1], chunk_of(1, chunk))
        p = jnp.exp2(s_s[item] - wide(stat[r]))
        ds = (p * (dp - wide(delta_s[r]))).astype(BF16)
        add_to(1, chunk, tn(p.astype(BF16), qg_s[r, 1]))
        dq_acc[r] += nn(ds, chunk_of(0, chunk))
        add_to(0, chunk, tn(ds, qg_s[r, 0]))

    for r in range(NZ):
        back(r, r, items[1, r])
    steps(back)

    od_s[:, 1] = (dq_acc[...] * scaling).astype(BF16)
    started += start_all([(od_s.at[:, 1], od_out.at[:, 1])], 1)
    dkvb[:, :, 0] = (dkv_s[:, :, 0] * scaling).astype(BF16)
    dkvb[:, :, 1] = dkv_s[:, :, 1].astype(BF16)
    copies = [
        (dkvb.at[pl.ds(0, 4), 1], first_out.at[pl.ds(0, 4)]),
        (dkvb.at[pl.ds(4, 2), 0], first_out.at[pl.ds(4, 2)]),
        (dkvb.at[pl.ds(8, 2), 1], third_out.at[pl.ds(0, 2)]),
        (dkvb.at[pl.ds(8, 2), 0], third_out.at[pl.ds(2, 2)]),
        (dkvb.at[pl.ds(4, 2), 1], later_third),
        (dkvb.at[pl.ds(6, 2), 1], later_first),
        (dkvb.at[pl.ds(6, 2), 0], across_out),
        (dkvb.at[pl.ds(0, 4), 0], own_out),
    ]
    for cp in started + start_all(copies, len(started)):
        cp.wait()


def attend(place, start, classes, lengths, qg, kvs, scaling):
    _, _, rows, width = qg.shape
    anywhere = pl.BlockSpec(memory_space=pl.ANY)
    scalars = pl.BlockSpec(memory_space=pltpu.SMEM)
    shape = lambda *lead: jax.ShapeDtypeStruct((*lead, width), BF16)
    slots = lambda kind: pltpu.VMEM((SLOTS, 2, 2, TB, width), kind)
    part = pltpu.VMEM((NZ, 2, rows, width), BF16)
    row = pltpu.VMEM((NZ, rows, TB), F32)
    outs = pl.pallas_call(
        functools.partial(attention_kernel, scaling=scaling),
        out_shape=[shape(NZ, 2, rows)]
        + [shape(n, 2, TB) for n in (4, 6, 4, 2, 2, 2)]
        + [jax.ShapeDtypeStruct((NZ,), jnp.int32)],
        in_specs=[scalars] * 3 + [pl.BlockSpec(memory_space=pltpu.VMEM)] + [anywhere] * 10,
        out_specs=[anywhere] * 7 + [scalars],
        scratch_shapes=[
            part,
            slots(BF16),
            pltpu.VMEM((MOST_ITEMS + UNROLL - 1, rows, CHUNK), F32),
            row,
            row,
            row,
            pltpu.VMEM((NZ, rows, 2 * width), F32),
            pltpu.VMEM((NZ, rows, width), F32),
            slots(F32),
            part,
            slots(BF16),
            pltpu.SMEM((3, MOST_ITEMS + UNROLL - 1), jnp.int32),
            pltpu.SemaphoreType.DMA((24,)),
        ],
        compiler_params=pltpu.CompilerParams(vmem_limit_bytes=60 * 2**20),
        cost_estimate=pl.CostEstimate(
            flops=16 * 12 * rows * CHUNK * width, bytes_accessed=10 * 2**20, transcendentals=0
        ),
        name="attend",
    )(place, start, classes, lengths.reshape(-1, 1), qg, *kvs)
    return outs[0], outs[1:7], outs[7]


def pick_kernel(place, key, value, *refs):
    outs, (scratch, sems) = refs[:NZ], refs[NZ:]
    copies = [
        pltpu.make_async_copy(ref, scratch.at[n], sems.at[n]) for n, ref in enumerate((key, value))
    ]
    for cp in copies:
        cp.start()
    z = place[0] >> 3
    groups = key.shape[1]
    for n in range(2):
        copies[n].wait()
        whole = scratch[n].astype(F32)
        kinds = [whole[:, g, :] for g in range(groups)]
        for r in range(NZ):
            piece = kinds[0]
            for g in range(1, groups):
                piece = jnp.where((z ^ r) * groups // NZ == g, kinds[g], piece)
            outs[r][n] = piece.astype(BF16)


def pick_groups(place, key, value):
    vmem = pl.BlockSpec(memory_space=pltpu.VMEM)
    return pl.pallas_call(
        pick_kernel,
        out_shape=[jax.ShapeDtypeStruct((2, key.shape[0], key.shape[2]), BF16)] * NZ,
        in_specs=[pl.BlockSpec(memory_space=pltpu.SMEM)] + [pl.BlockSpec(memory_space=pl.ANY)] * 2,
        out_specs=[vmem] * NZ,
        scratch_shapes=[pltpu.VMEM((2, *key.shape), BF16), pltpu.SemaphoreType.DMA((2,))],
        compiler_params=pltpu.CompilerParams(vmem_limit_bytes=4 * 2**20),
        cost_estimate=pl.CostEstimate(flops=0, bytes_accessed=2**19, transcendentals=0),
        name="pick_groups",
    )(place, key, value)


def arrange_kernel(place, first_tile, *refs):
    parts, (whole, chosen), sems = refs[:NZ], refs[NZ : NZ + 2], refs[NZ + 2]
    me, start = place[0], first_tile[0]
    z, y, x = me >> 3, (me >> 2) & 1, me & 3
    order = layers(start, y, x)
    copies = []
    for r in range(NZ):
        there = z ^ r
        spot = sum(jnp.where(there == order[n], n, 0) for n in range(1, NZ))
        copies.append(pltpu.make_async_copy(parts[r], whole.at[spot], sems.at[r]))
        copies[-1].start()
        picked = (there == order[2]) | (there == order[3])

        @pl.when(picked)
        def _(r=r, spot=spot):
            cp = pltpu.make_async_copy(parts[r], chosen.at[jnp.maximum(spot - 2, 0)], sems.at[NZ])
            cp.start()
            cp.wait()

    for cp in copies:
        cp.wait()


def arrange(place, start, parts):
    shape = lambda n: jax.ShapeDtypeStruct((n, *parts[0].shape), BF16)
    return pl.pallas_call(
        arrange_kernel,
        out_shape=[shape(4), shape(2)],
        in_specs=[pl.BlockSpec(memory_space=pltpu.SMEM)] * 2
        + [pl.BlockSpec(memory_space=pltpu.VMEM)] * NZ,
        out_specs=[pl.BlockSpec(memory_space=pl.ANY)] * 2,
        scratch_shapes=[pltpu.SemaphoreType.DMA((NZ + 1,))],
        compiler_params=pltpu.CompilerParams(vmem_limit_bytes=4 * 2**20),
        cost_estimate=pl.CostEstimate(flops=0, bytes_accessed=2**19, transcendentals=0),
        name="arrange",
    )(place, start, *parts)


def split_kernel(sizes, query, cotangent, out, first_tile):
    first_tile[0] = long_start(sizes)
    share = query.shape[1] // NZ
    for c in range(NZ):
        for n, ref in enumerate((query, cotangent)):
            piece = ref[:, share * c : share * (c + 1), :].astype(F32)
            out[c, n] = piece.reshape(out.shape[2:]).astype(BF16)


def split_heads(lengths, query, cotangent):
    count, heads, width = query.shape
    vmem, scalars = pl.BlockSpec(memory_space=pltpu.VMEM), pl.BlockSpec(memory_space=pltpu.SMEM)
    return pl.pallas_call(
        split_kernel,
        out_shape=[
            jax.ShapeDtypeStruct((NZ, 2, count * heads // NZ, width), BF16),
            jax.ShapeDtypeStruct((1,), jnp.int32),
        ],
        in_specs=[scalars, vmem, vmem],
        out_specs=[vmem, scalars],
        compiler_params=pltpu.CompilerParams(vmem_limit_bytes=24 * 2**20),
        cost_estimate=pl.CostEstimate(flops=0, bytes_accessed=4 * 2**20, transcendentals=0),
        name="split_heads",
    )(lengths, query, cotangent)


def join_kernel(parts, *outs):
    count, heads, width = outs[0].shape
    for n, out in enumerate(outs):
        pieces = [parts[c, n].astype(F32).reshape(count, heads // NZ, width) for c in range(NZ)]
        out[...] = jnp.concatenate(pieces, axis=1).astype(BF16)


def join_heads(parts, shape):
    return pl.pallas_call(
        join_kernel,
        out_shape=[jax.ShapeDtypeStruct(shape, BF16)] * 2,
        compiler_params=pltpu.CompilerParams(vmem_limit_bytes=24 * 2**20),
        cost_estimate=pl.CostEstimate(flops=0, bytes_accessed=4 * 2**20, transcendentals=0),
        name="join_heads",
    )(parts)


def swap(a, mask):
    return lax.ppermute(a, "ctx", [(i, i ^ mask) for i in range(CTX)])


def along_z(a, r):
    return swap(a, 8 * r)


def exchange_z(a):
    groups = [list(range(first, CTX, NY * NX)) for first in range(NY * NX)]
    return lax.all_to_all(a, "ctx", 0, 0, axis_index_groups=groups, tiled=True)


def along_x(a, r):
    return swap(a, r)


def along_y(a):
    return swap(a, NX)


def add_up(*parts):
    total = parts[0].astype(F32)
    for part in parts[1:]:
        total = total + part.astype(F32)
    return total


def on_device(query, key, value, grad_out, doc_lengths, tile_class):
    groups = key.shape[1]
    width = query.shape[2]
    scaling = width ** (-0.5)
    place = lax.axis_index("ctx")
    z = place // 8

    here = place.reshape(1).astype(jnp.int32)

    others = (1, 2, 3)
    kv = pick_groups(here, key, value)
    qg, start = split_heads(doc_lengths, query, grad_out)
    kv = [kv[0]] + [along_z(kv[r], r) for r in others]
    whole, chosen = arrange(here, start, kv)
    chosen, qg = lax.optimization_barrier((chosen, qg))
    qg = exchange_z(qg)
    across = along_y(chosen)
    first = along_x(jnp.concatenate((whole, across)), 1)
    third = along_x(jnp.concatenate((chosen, across)), 3)
    far, further = along_x(third[:2], 1), along_x(first[4:], 3)

    od, dkvs, layer = attend(
        here, start, tile_class, doc_lengths, qg, [*kv, first, third, far, further, across], scaling
    )

    own, to_first, to_third, later_third, later_first, own_across = dkvs
    from_first, from_third = along_x(to_first, 1), along_x(to_third, 3)
    od = exchange_z(od)
    to_third = add_up(later_third, from_first[4:]).astype(BF16)
    to_first = add_up(later_first, from_third[2:]).astype(BF16)
    more, more_across = along_x(to_third, 3), along_x(to_first, 1)
    across = along_y(add_up(own_across, from_third[:2], more_across).astype(BF16))
    chosen = add_up(more, across)
    layer = layer[:, None, None, None]
    dkv = add_up(own, from_first[:4]) + jnp.where(
        layer == 0, chosen[0], jnp.where(layer == 1, chosen[1], 0.0)
    )
    parts = [dkv[0]] + [along_z(dkv[r].astype(BF16), r).astype(F32) for r in others]
    attention, grad_query = join_heads(od, query.shape)
    mine = (parts[0] + parts[1]).astype(BF16)[:, :, None, :]
    other = (parts[2] + parts[3]).astype(BF16)[:, :, None, :]
    group = lax.broadcasted_iota(jnp.int32, (1, 1, groups, 1), 2)
    grads = jnp.where(group == z * groups // NZ, mine, other)
    return attention, grad_query, grads[0], grads[1]


def solution(mesh):
    spec = P("ctx", "heads", None)
    return jax.shard_map(
        on_device,
        mesh=mesh,
        in_specs=(spec, spec, spec, spec, P(), P()),
        out_specs=(spec, spec, spec, spec),
        check_vma=False,
    )
```
